32 devices in a mesh: groups: 2 (over y), sector: 16 (over z, x, core).
Axes of the slice: x: 2, y: 2, z: 4, core: 2. Of those that a mesh axis runs over, the one named last changes fastest.
Arguments:
- psi: bfloat16 [512, 128, 128], P(('groups', 'sector')), parts along dimension 0, may hold values from -6 to 6
- left_env: bfloat16 [32, 30, 128, 128], P(('groups', 'sector')), parts along dimension 0, may hold values from -0.5 to 0.5
- right_env: bfloat16 [32, 30, 128, 128], P(('groups', 'sector')), parts along dimension 0, may hold values from -0.09375 to 0.09375
- mpo: bfloat16 [32, 30, 30], P('groups'), parts along dimension 0, may hold values from -1 to 1
- block_target: int32 [512, 1], P(('groups', 'sector')), parts along dimension 0, may hold values from 0 to 7; in each aligned block of 16 rows (0 to 15, 16 to 31, ...) at most 2 rows name the same one
- block_phys: int32 [512], P(('groups', 'sector')), parts along dimension 0, may hold values from 0 to 15
Outputs:
- hpsi: bfloat16 [512, 128, 128], P(('groups', 'sector')), parts along dimension 0
The draws below stay inside these ranges and needn't reach their ends.
There are 2 independent parts, one for each index of `groups`. The reference program is written for one: setup_inputs(seed, part) draws one part's arguments, and reference() takes and returns one part's arrays. A program takes and returns all parts, laid end to end along the dimension named above; each array names one. Nothing has to cross between parts.
Inputs may be any that keep to these rules, and one draw needn't show every extreme that they name: `block_target`: among the 16 blocks of one left sector, no offset is named by more than 2 blocks.
All inputs are finite; a program needn't handle non-finite values.
Results may differ from the reference program's by a relative error of at most 0.0057.
Values may be sent and summed in bfloat16 or wider, within the bound.
A program may use at most 192 MiB of HBM per device.

```python
import math
import jax
import jax.numpy as jnp
import numpy as np
from jax import lax

BS = 128
W = 30
NPH = 16
SPREAD = 8
CAP = 2
BLK_DEV = 16
SECTORS = 16
BLOCKS = 256


def set_ends(drawn, key, low, top_value):
    longest = drawn.shape.index(max(drawn.shape))
    spots = []
    for shift in (0, 1):
        where = [jax.random.randint(jax.random.fold_in(key, axis), (), 0, length) for axis, length in enumerate(drawn.shape)]
        where[longest] = (where[longest] + shift) % drawn.shape[longest]
        spots.append(tuple(where))
    return drawn.at[spots[0]].set(low).at[spots[1]].set(top_value)


def level_of(rng, shape, split, smallest, largest):
    level = 1.0
    for axis_at, blocks in split:
        draws = jax.random.uniform(jax.random.fold_in(jax.random.fold_in(rng, 6), axis_at), (blocks,), jnp.float32, smallest / len(split), largest / len(split))
        level = level * jnp.repeat(jnp.exp(draws), shape[axis_at] // blocks).reshape((-1,) + (1,) * (len(shape) - 1 - axis_at))
    return level


def assign_block(rng, own, number, rows, number_of, top, limit, lean):
    order = jax.random.permutation(rng, number_of)
    packed, usual = portions_of(number_of, rows * top, limit, lean, True), portions_of(number_of, rows * top, limit, lean, False)
    places = jnp.arange(number_of)

    def named(tallies, rotation):
        used = int((tallies > 0).sum())
        fixed = max(1, used // 4)
        passed = fixed + (places - fixed + rotation * (used - fixed)) % max(1, number_of - fixed)
        return jnp.zeros((number_of,), jnp.int32).at[order[jnp.where(places < fixed, places, passed)]].set(jnp.asarray(tallies, jnp.int32))

    tallies = jnp.where(number % 4 == 0, named(packed, number // 4), named(usual, number - number // 4 - 1))
    mixed = jax.random.permutation(jax.random.fold_in(own, 3), number_of)
    source_of, receiver = mixed[0:number_of // 2 * 2:2], mixed[1:number_of // 2 * 2:2]
    room = jnp.minimum(tallies[source_of] - 1, limit - tallies[receiver]) // 2
    room = jnp.where((source_of == order[0]) | (receiver == order[0]) | (tallies[receiver] == 0), 0, jnp.maximum(room, 0))
    passed = jax.random.randint(jax.random.fold_in(own, 4), (number_of // 2,), 0, 1 << 20) % (room + 1)
    tallies = tallies.at[source_of].add(-passed).at[receiver].add(passed)
    members = jnp.searchsorted(jnp.cumsum(tallies), jnp.arange(rows * top), side="right").astype(jnp.int32)
    grid = members.reshape(top, rows).T
    grid = grid[jax.random.permutation(jax.random.fold_in(own, 1), rows)]
    rotation = jax.random.randint(jax.random.fold_in(own, 2), (rows, 1), 0, top)
    return jnp.take_along_axis(grid, (jnp.arange(top)[None, :] + rotation) % top, axis=1)


def portions_of(amount, total, bound, skew, full):
    loads = [(1 << 20) // math.isqrt(rank ** skew) + 1 for rank in range(1, amount + 1)]
    largest = bound if full else min(bound, max(-(-total // amount), total * loads[0] // sum(loads)))
    least = 1 if total - largest >= amount - 1 else 0
    given, spare = [largest] + [least] * (amount - 1), total - largest - least * (amount - 1)
    while spare > 0:
        candidates = [i for i in range(1, amount) if given[i] < largest] or [i for i in range(1, amount) if given[i] < bound]
        whole, left = sum([loads[i] for i in candidates]), spare
        for i in candidates:
            more = min(bound - given[i], max(1, left * loads[i] // whole), spare)
            given[i] = given[i] + more
            spare = spare - more
    return np.array(given)


def scatter_about(key, extent, scale, limit, split=(), held_as=jnp.bfloat16):
    values = scale * jax.random.normal(key, extent, jnp.float32)
    if split:
        values = values * level_of(key, extent, split, -0.22, 0.18)
    return jnp.clip(values, -limit, limit).astype(held_as)


def setup_inputs(seed: int = 0, part: int = 0) -> dict:
    seeds = jax.random.split(jax.random.key(seed), 7)
    own_keys = jax.random.split(jax.random.fold_in(seeds[6], part), 7)
    psi = scatter_about(own_keys[0], (BLOCKS, BS, BS), 1.0, 6.0, ((0, 16),))
    left_env = scatter_about(own_keys[1], (SECTORS, W, BS, BS), BS ** -0.5, 0.5, ((0, 16),))
    right_env = scatter_about(own_keys[2], (SECTORS, W, BS, BS), (W * BS) ** -0.5, 0.09375, ((0, 16),))
    mpo = scatter_about(own_keys[3], (NPH, W, W), W ** -0.5, 1.0)
    block_target_keys = jax.random.split(jax.random.fold_in(own_keys[4], 1), BLOCKS // BLK_DEV)
    block_target_turns = jax.random.permutation(jax.random.fold_in(own_keys[4], 3), BLOCKS // BLK_DEV)
    block_target = jax.vmap(lambda own, number: assign_block(jax.random.fold_in(own_keys[4], 2), own, number, BLK_DEV, SPREAD, 1, CAP, 1))(block_target_keys, block_target_turns).reshape((BLOCKS, 1))
    block_phys = set_ends(jax.random.randint(own_keys[5], (BLOCKS,), 0, NPH), jax.random.fold_in(own_keys[5], 1), 0, NPH - 1).astype(jnp.int32)
    return dict(psi=psi, left_env=left_env, right_env=right_env, mpo=mpo, block_target=block_target, block_phys=block_phys)


def reference(psi, left_env, right_env, mpo, block_target, block_phys):
    owners = jnp.arange(BLOCKS, dtype=jnp.int32) // BLK_DEV
    targets = (owners + block_target[:, 0]) % SECTORS

    def single(items):
        block, owner, target, label = items
        lenv = left_env[owner].astype(jnp.float32)
        contracted = jnp.einsum("wab,bc->wac", lenv, block.astype(jnp.float32)).astype(jnp.bfloat16)
        weights = mpo[label].astype(jnp.float32)
        mixed = jnp.einsum("wac,wv->avc", contracted.astype(jnp.float32), weights).astype(jnp.bfloat16)
        renv = right_env[target].reshape(W * BS, BS)
        result = jnp.dot(mixed.reshape(BS, W * BS), renv, preferred_element_type=jnp.float32)
        return result.astype(jnp.bfloat16)

    return lax.map(single, (psi, owners, targets, block_phys))
```

```python
import functools

import jax
import jax.numpy as jnp
from jax import lax
from jax.experimental import pallas as pl
from jax.experimental.pallas import tpu as pltpu
from jax.sharding import PartitionSpec as P

SPREAD = 8
CAP = 2
LEVEL = 4
CHUNKS = 3
SUB = 8

OWN = (
    (0, 0, 1, 0), (1, 1, 1, 1), (2, 2, 1, 2), (3, 3, 1, 3),
    (2, 2, 0, 0), (3, 3, 0, 1), (1, 1, 0, 0), (3, 3, 0, 2),
)
FIRST = (
    (0, 4, 0, 2), (0, 4, 1, 1), (0, 4, 0, 1), (0, 2, 0, 1),
    (1, 5, 0, 3), (1, 5, 0, 0), (1, 3, 0, 0),
    (2, 6, 1, 3), (2, 6, 0, 0), (2, 6, 0, 3),
    (3, 7, 0, 1), (3, 7, 0, 2),
)
ACROSS = ((2, 4, 0, 3), (3, 5, 1, 2), (3, 5, 0, 2))
SECOND = (
    (1, 8, 0, 2), (0, 6, 0, 1), (1, 7, 0, 0), (2, 8, 0, 3), (2, 9, 0, 3),
)
MOVES = OWN + FIRST + ACROSS + SECOND


def kernel(
    count, bond, width, target_ref, phys_ref, psi_ref, left_ref, right_ref, mpo_ref, out_ref,
    envs, mixed, left_tiles, weights, done, order, send_sem, recv_sem, own_sem,
):
    nblock = psi_ref.shape[0]
    depth = bond * width
    part = depth // CHUNKS
    rows = bond * SUB
    padded = left_tiles.shape[1]
    group = lax.axis_index("groups")
    me = lax.axis_index("sector")
    role = lax.rem(me, LEVEL)
    base = me - role
    below = lax.rem(base + count - LEVEL, count)
    above = lax.rem(base + LEVEL, count)

    own_copy = pltpu.make_async_copy(right_ref, envs.at[0], own_sem)
    own_copy.start()

    barrier = pltpu.get_barrier_semaphore()
    for step in range(1, LEVEL):
        pl.semaphore_signal(
            barrier, inc=1, device_id=(group, base + lax.rem(role + step, LEVEL)),
            device_id_type=pl.DeviceIdType.MESH,
        )
    for place in range(LEVEL):
        for start in (below, above):
            pl.semaphore_signal(
                barrier, inc=1, device_id=(group, start + place),
                device_id_type=pl.DeviceIdType.MESH,
            )
    pl.semaphore_wait(barrier, 3 * LEVEL - 1)

    def moving(move, chunk):
        holder, i, down, target = move
        number = [m for m in MOVES if m[0] == holder].index(move)
        piece = pl.ds(chunk * part, part)
        place = i + LEVEL * down - target
        source = right_ref.at[piece] if i == holder else envs.at[i - holder, piece]
        return pltpu.make_async_remote_copy(
            src_ref=source,
            dst_ref=envs.at[place, piece],
            send_sem=send_sem.at[number, chunk],
            recv_sem=recv_sem.at[place, chunk],
            device_id=(group, (below if down else base) + target),
            device_id_type=pl.DeviceIdType.MESH,
        )

    def arrived(holder, i, chunk):
        piece = envs.at[i - holder, pl.ds(chunk * part, part)]
        pltpu.make_async_remote_copy(
            src_ref=piece,
            dst_ref=piece,
            send_sem=send_sem.at[0, chunk],
            recv_sem=recv_sem.at[i - holder, chunk],
            device_id=(group, below + holder),
            device_id_type=pl.DeviceIdType.MESH,
        ).wait_recv()

    def pass_on(moves, chunk):
        for holder in range(LEVEL):
            mine = [m for m in moves if m[0] == holder]
            if mine:

                @pl.when(role == holder)
                def _():
                    seen = set()
                    for move in mine:
                        if move[1] != holder and move[1] not in seen:
                            arrived(holder, move[1], chunk)
                        seen.add(move[1])
                        moving(move, chunk).start()

    for chunk in range(CHUNKS):
        pass_on(OWN, chunk)

    for offset in range(SPREAD):
        first = jnp.int32(nblock)
        last = jnp.int32(0)
        for k in range(nblock):
            same = target_ref[k] == offset
            first = jnp.where(same, jnp.minimum(first, k), first)
            last = jnp.where(same, k, last)
        order[CAP * offset] = jnp.minimum(first, nblock - 1)
        order[CAP * offset + 1] = last

    for tile in range(width // (2 * SUB)):
        both = left_ref[:, 2 * SUB * tile : 2 * SUB * (tile + 1), :].astype(jnp.float32)
        for half in range(2):
            slab = both[:, SUB * half : SUB * (half + 1), :].reshape(rows, width)
            left_tiles[2 * tile + half, :rows, :] = slab.astype(jnp.bfloat16)
            if padded > rows:
                left_tiles[2 * tile + half, rows:, :] = jnp.zeros(
                    (padded - rows, width), jnp.bfloat16
                )

    row_of = lax.broadcasted_iota(jnp.int32, (rows, bond), 0) // SUB
    spread_rows = (row_of == lax.broadcasted_iota(jnp.int32, (rows, bond), 1)).astype(jnp.bfloat16)
    lane_of = lax.broadcasted_iota(jnp.int32, (bond, padded), 1) // SUB
    spread_lanes = (lane_of == lax.broadcasted_iota(jnp.int32, (bond, padded), 0)).astype(
        jnp.bfloat16
    )

    def mix_pair(offset):
        blocks = [order[CAP * offset + p] for p in range(CAP)]
        for p in range(CAP):
            element = mpo_ref[phys_ref[blocks[p]]]
            tall = lax.dot_general(
                spread_rows, element, (((1,), (1,)), ((), ())),
                preferred_element_type=jnp.float32,
            ).astype(jnp.bfloat16)
            wide = jnp.dot(tall, spread_lanes, preferred_element_type=jnp.float32)
            shape = (rows, padded)
            diagonal = lax.rem(lax.broadcasted_iota(jnp.int32, shape, 0), SUB) == lax.rem(
                lax.broadcasted_iota(jnp.int32, shape, 1), SUB
            )
            weights[p] = jnp.where(diagonal, wide, 0.0).astype(jnp.bfloat16)
        both = jnp.concatenate([psi_ref[block] for block in blocks], axis=1)

        def tile_step(tile, carry):
            slabs = left_tiles[pl.ds(2 * tile, 2)].reshape(2 * padded, width)
            contracted = jnp.dot(slabs, both, preferred_element_type=jnp.float32).astype(
                jnp.bfloat16
            )
            for p in range(CAP):
                columns = slice(p * width, (p + 1) * width)
                pair = jnp.concatenate(
                    [contracted[:padded, columns], contracted[padded:, columns]], axis=1
                )
                product = jnp.dot(weights[p], pair, preferred_element_type=jnp.float32)
                tiles = jnp.concatenate(
                    [
                        product[:, :width].reshape(bond, SUB, width),
                        product[:, width:].reshape(bond, SUB, width),
                    ],
                    axis=1,
                ).astype(jnp.bfloat16)
                at = pl.ds(pl.multiple_of(p * width + tile * 2 * SUB, 2 * SUB), 2 * SUB)
                for v in range(bond):
                    mixed[offset, at, v * width : (v + 1) * width] = tiles[v]
            return carry

        lax.fori_loop(0, width // (2 * SUB), tile_step, 0)

    def mix_pairs(begin, end):
        def step(offset, carry):
            mix_pair(offset)
            return carry

        lax.fori_loop(begin, end, step, 0)

    passed = {(m[0], m[1]) for m in MOVES}

    def finish(offset):
        if offset == 0:
            own_copy.wait()
        else:
            for holder in range(LEVEL):
                if (holder, holder + offset) not in passed:

                    @pl.when(role == holder)
                    def _():
                        for chunk in range(CHUNKS):
                            arrived(holder, holder + offset, chunk)

        result = jnp.dot(mixed[offset], envs[offset], preferred_element_type=jnp.float32)
        done[pl.ds(CAP * offset, CAP)] = result.reshape(CAP, width, width).astype(jnp.bfloat16)

    mix_pairs(0, 2)
    pass_on(FIRST, 0)
    mix_pairs(2, 4)
    pass_on(FIRST, 1)
    pass_on(ACROSS, 0)
    mix_pairs(4, 6)
    pass_on(FIRST, 2)
    pass_on(ACROSS, 1)
    mix_pairs(6, SPREAD)
    pass_on(ACROSS, 2)
    finish(0)
    finish(1)
    pass_on(SECOND, 0)
    finish(2)
    finish(3)
    pass_on(SECOND, 1)
    finish(4)
    pass_on(SECOND, 2)
    for offset in range(5, SPREAD):
        finish(offset)

    for k in range(nblock):
        earlier = jnp.int32(0)
        for other in range(k):
            earlier = jnp.where(target_ref[other] == target_ref[k], 1, earlier)
        out_ref[k] = done[CAP * target_ref[k] + earlier]

    for holder in range(LEVEL):

        @pl.when(role == holder)
        def _():
            for move in MOVES:
                if move[0] == holder:
                    for chunk in range(CHUNKS):
                        moving(move, chunk).wait_send()


def per_device(count, psi, left_env, right_env, mpo, block_target, block_phys):
    nblock, width, _ = psi.shape
    bond = left_env.shape[1]
    depth = bond * width
    padded = -(-bond * SUB // 256) * 256
    sends = max(sum(m[0] == holder for m in MOVES) for holder in range(LEVEL))
    in_vmem = pl.BlockSpec(memory_space=pltpu.VMEM)
    in_smem = pl.BlockSpec(memory_space=pltpu.SMEM)
    return pl.pallas_call(
        functools.partial(kernel, count, bond, width),
        out_shape=jax.ShapeDtypeStruct((nblock, width, width), jnp.bfloat16),
        in_specs=[
            in_smem, in_smem, in_vmem, in_vmem, pl.BlockSpec(memory_space=pl.ANY), in_vmem,
        ],
        out_specs=in_vmem,
        scratch_shapes=[
            pltpu.VMEM((SPREAD, depth, width), jnp.bfloat16),
            pltpu.VMEM((SPREAD, CAP * width, depth), jnp.bfloat16),
            pltpu.VMEM((width // SUB, padded, width), jnp.bfloat16),
            pltpu.VMEM((CAP, bond * SUB, padded), jnp.bfloat16),
            pltpu.VMEM((nblock, width, width), jnp.bfloat16),
            pltpu.SMEM((CAP * SPREAD,), jnp.int32),
            pltpu.SemaphoreType.DMA((sends, CHUNKS)),
            pltpu.SemaphoreType.DMA((SPREAD, CHUNKS)),
            pltpu.SemaphoreType.DMA,
        ],
        compiler_params=pltpu.CompilerParams(
            collective_id=0, has_side_effects=True, vmem_limit_bytes=48 * 1024 * 1024
        ),
        name="hamiltonian_product",
    )(
        block_target.reshape(nblock), block_phys, psi, left_env.reshape(bond, width, width),
        right_env.reshape(depth, width), mpo,
    )


def solution(mesh):
    in_specs = (
        P(("groups", "sector"), None, None),
        P(("groups", "sector"), None, None, None),
        P(("groups", "sector"), None, None, None),
        P("groups", None, None),
        P(("groups", "sector"), None),
        P(("groups", "sector")),
    )
    out_specs = P(("groups", "sector"), None, None)
    return jax.shard_map(
        functools.partial(per_device, mesh.shape["sector"]),
        mesh=mesh, in_specs=in_specs, out_specs=out_specs, check_vma=False,
    )
```

```python
import functools

import jax
import jax.numpy as jnp
from jax import lax
from jax.experimental import pallas as pl
from jax.experimental.pallas import tpu as pltpu
from jax.sharding import PartitionSpec as P

SPREAD = 8
CAP = 2
LEVEL = 4
CHUNKS = 10
SUB = 8

ALL, EARLY, LATE = 0, 1, 2
OWN = (
    (0, 0, 1, 0, ALL), (1, 1, 1, 1, ALL), (2, 2, 1, 2, ALL), (3, 3, 1, 3, LATE),
    (2, 2, 0, 0, ALL), (3, 3, 0, 1, ALL), (1, 1, 0, 0, ALL), (3, 3, 0, 2, ALL),
)
FIRST = (
    (0, 4, 0, 2, ALL), (0, 4, 1, 1, ALL), (0, 4, 0, 1, ALL), (0, 2, 0, 1, ALL),
    (1, 5, 0, 3, ALL), (1, 5, 0, 0, ALL), (1, 3, 1, 1, EARLY), (1, 3, 0, 0, ALL),
    (2, 6, 0, 0, ALL), (2, 6, 1, 3, ALL), (2, 6, 0, 3, ALL),
    (3, 7, 0, 1, LATE), (3, 7, 0, 2, LATE),
)
ACROSS = ((2, 4, 0, 3, ALL), (3, 5, 1, 2, ALL), (3, 5, 0, 2, ALL))
SECOND = (
    (1, 8, 0, 2, ALL), (1, 7, 0, 3, EARLY), (1, 7, 0, 0, ALL), (0, 6, 0, 1, ALL),
    (2, 8, 0, 3, ALL), (2, 9, 0, 3, ALL), (3, 7, 0, 2, EARLY),
)
MOVES = OWN + FIRST + ACROSS + SECOND


def applies(move, chunk):
    return move[4] == ALL or (chunk < CHUNKS // 2) == (move[4] == EARLY)


def kernel(
    count, bond, width, target_ref, phys_ref, psi_hbm, left_hbm, right_ref, mpo_hbm, out_ref,
    psi_ref, left_ref, mpo_ref, envs, mixed, left_tiles, weights, held, done, order, send_sem, recv_sem, own_sem, load_sem,
):
    nblock = psi_ref.shape[0]
    depth = bond * width
    part = depth // CHUNKS
    rows = bond * SUB
    padded = left_tiles.shape[1]
    group = lax.axis_index("groups")
    me = lax.axis_index("sector")
    role = lax.rem(me, LEVEL)
    base = me - role
    below = lax.rem(base + count - LEVEL, count)
    above = lax.rem(base + LEVEL, count)

    own_copy = pltpu.make_async_copy(right_ref, envs.at[0], own_sem)
    loads = [
        pltpu.make_async_copy(source, target, load_sem.at[n])
        for n, (source, target) in enumerate(
            ((left_hbm, left_ref), (mpo_hbm, mpo_ref), (psi_hbm, psi_ref))
        )
    ]
    for load in loads:
        load.start()
    own_copy.start()

    barrier = pltpu.get_barrier_semaphore()
    for step in range(1, LEVEL):
        pl.semaphore_signal(
            barrier, inc=1, device_id=(group, base + lax.rem(role + step, LEVEL)),
            device_id_type=pl.DeviceIdType.MESH,
        )
    for place in range(LEVEL):
        for start in (below, above):
            pl.semaphore_signal(
                barrier, inc=1, device_id=(group, start + place),
                device_id_type=pl.DeviceIdType.MESH,
            )
    pl.semaphore_wait(barrier, 3 * LEVEL - 1)

    def moving(move, chunk):
        holder, i, down, target, _ = move
        number = [m for m in MOVES if m[0] == holder].index(move)
        piece = pl.ds(chunk * part, part)
        place = i + LEVEL * down - target
        source = right_ref.at[piece] if i == holder else envs.at[i - holder, piece]
        return pltpu.make_async_remote_copy(
            src_ref=source,
            dst_ref=envs.at[place, piece],
            send_sem=send_sem.at[number, chunk],
            recv_sem=recv_sem.at[place, chunk],
            device_id=(group, (below if down else base) + target),
            device_id_type=pl.DeviceIdType.MESH,
        )

    def arrived(holder, i, chunk):
        piece = envs.at[i - holder, pl.ds(chunk * part, part)]
        pltpu.make_async_remote_copy(
            src_ref=piece,
            dst_ref=piece,
            send_sem=send_sem.at[0, chunk],
            recv_sem=recv_sem.at[i - holder, chunk],
            device_id=(group, below + holder),
            device_id_type=pl.DeviceIdType.MESH,
        ).wait_recv()

    def pass_on(moves, chunk):
        for holder in range(LEVEL):
            mine = [m for m in moves if m[0] == holder and applies(m, chunk)]
            if mine:

                @pl.when(role == holder)
                def _():
                    seen = set()
                    for move in mine:
                        if move[1] != holder and move[1] not in seen:
                            arrived(holder, move[1], chunk)
                        seen.add(move[1])
                        moving(move, chunk).start()

    for chunk in range(CHUNKS):
        pass_on(OWN, chunk)

    for offset in range(SPREAD):
        first = jnp.int32(nblock)
        last = jnp.int32(0)
        for k in range(nblock):
            same = target_ref[k] == offset
            first = jnp.where(same, jnp.minimum(first, k), first)
            last = jnp.where(same, k, last)
        order[CAP * offset] = jnp.minimum(first, nblock - 1)
        order[CAP * offset + 1] = last

    for load in loads:
        load.wait()

    for tile in range(width // (2 * SUB)):
        both = left_ref[:, 2 * SUB * tile : 2 * SUB * (tile + 1), :].astype(jnp.float32)
        for half in range(2):
            slab = both[:, SUB * half : SUB * (half + 1), :].reshape(rows, width)
            left_tiles[2 * tile + half, :rows, :] = slab.astype(jnp.bfloat16)
            if padded > rows:
                left_tiles[2 * tile + half, rows:, :] = jnp.zeros(
                    (padded - rows, width), jnp.bfloat16
                )

    row_of = lax.broadcasted_iota(jnp.int32, (rows, bond), 0) // SUB
    spread_rows = (row_of == lax.broadcasted_iota(jnp.int32, (rows, bond), 1)).astype(jnp.bfloat16)
    lane_of = lax.broadcasted_iota(jnp.int32, (bond, padded), 1) // SUB
    spread_lanes = (lane_of == lax.broadcasted_iota(jnp.int32, (bond, padded), 0)).astype(
        jnp.bfloat16
    )

    shape = (rows, padded)
    diagonal = lax.rem(lax.broadcasted_iota(jnp.int32, shape, 0), SUB) == lax.rem(
        lax.broadcasted_iota(jnp.int32, shape, 1), SUB
    )

    def spread_element(at, carry):
        element = mpo_ref[phys_ref[order[at]]]
        tall = lax.dot_general(
            spread_rows, element, (((1,), (1,)), ((), ())), preferred_element_type=jnp.float32
        ).astype(jnp.bfloat16)
        wide = jnp.dot(tall, spread_lanes, preferred_element_type=jnp.float32)
        weights[at] = jnp.where(diagonal, wide, 0.0).astype(jnp.bfloat16)
        return carry

    def spread_elements(begin, end):
        lax.fori_loop(begin, end, spread_element, 0, unroll=2)

    tiles = width // (2 * SUB)

    def contract(offset, tile, slot):
        both = jnp.concatenate([psi_ref[order[CAP * offset + p]] for p in range(CAP)], axis=1)
        slabs = left_tiles[pl.ds(2 * tile, 2)].reshape(2 * padded, width)
        held[slot] = jnp.dot(slabs, both, preferred_element_type=jnp.float32).astype(
            jnp.bfloat16
        )

    def mix(offset, tile, slot):
        for p in range(CAP):
            columns = slice(p * width, (p + 1) * width)
            pair = jnp.concatenate(
                [held[slot, :padded, columns], held[slot, padded:, columns]], axis=1
            )
            product = jnp.dot(
                weights[CAP * offset + p], pair, preferred_element_type=jnp.float32
            )
            stacked = jnp.concatenate(
                [
                    product[:, :width].reshape(bond, SUB, width),
                    product[:, width:].reshape(bond, SUB, width),
                ],
                axis=1,
            ).astype(jnp.bfloat16)
            at = pl.ds(pl.multiple_of(p * width + tile * 2 * SUB, 2 * SUB), 2 * SUB)
            for v in range(bond):
                mixed[offset, at, v * width : (v + 1) * width] = stacked[v]

    total_steps = SPREAD * tiles

    def mix_steps(begin, end):
        def step(n, carry):
            for half in range(2):
                now = 2 * n + half
                after = jnp.minimum(now + 1, total_steps - 1)
                contract(after // tiles, lax.rem(after, tiles), 1 - half)
                mix(now // tiles, lax.rem(now, tiles), half)
            return carry

        lax.fori_loop(begin * tiles // 4, end * tiles // 4, step, 0)

    passed = {(m[0], m[1]) for m in MOVES}

    def finish(offset):
        if offset == 0:
            own_copy.wait()
        else:
            for holder in range(LEVEL):
                if (holder, holder + offset) not in passed:

                    @pl.when(role == holder)
                    def _():
                        for chunk in range(CHUNKS):
                            arrived(holder, holder + offset, chunk)

        result = jnp.dot(mixed[offset], envs[offset], preferred_element_type=jnp.float32)
        done[pl.ds(CAP * offset, CAP)] = result.reshape(CAP, width, width).astype(jnp.bfloat16)

    def phase(n):
        if n < CHUNKS:
            pass_on(FIRST, n)
        if 0 < n <= CHUNKS:
            pass_on(ACROSS, n - 1)

    spread_elements(0, CAP * SPREAD // 2)
    phase(0)
    spread_elements(CAP * SPREAD // 2, CAP * SPREAD)
    contract(0, 0, 0)
    stages = 2 * SPREAD
    for stage in range(stages):
        mix_steps(stage, stage + 1)
        for n in range(1, CHUNKS + 1):
            if (n - 1) * stages // CHUNKS == stage:
                phase(n)
    for chunk in range(CHUNKS):
        pass_on(SECOND, chunk)
        if chunk < 4:
            finish(chunk)
        elif chunk == CHUNKS // 2:
            finish(4)
    for offset in range(5, SPREAD):
        finish(offset)

    for k in range(nblock):
        earlier = jnp.int32(0)
        for other in range(k):
            earlier = jnp.where(target_ref[other] == target_ref[k], 1, earlier)
        out_ref[k] = done[CAP * target_ref[k] + earlier]

    for holder in range(LEVEL):

        @pl.when(role == holder)
        def _():
            for move in MOVES:
                if move[0] == holder:
                    for chunk in range(CHUNKS):
                        if applies(move, chunk):
                            moving(move, chunk).wait_send()


def per_device(count, psi, left_env, right_env, mpo, block_target, block_phys):
    nblock, width, _ = psi.shape
    bond = left_env.shape[1]
    depth = bond * width
    padded = -(-bond * SUB // 256) * 256
    sends = max(sum(m[0] == holder for m in MOVES) for holder in range(LEVEL))
    in_vmem = pl.BlockSpec(memory_space=pltpu.VMEM)
    in_place = pl.BlockSpec(memory_space=pl.ANY)
    in_smem = pl.BlockSpec(memory_space=pltpu.SMEM)
    return pl.pallas_call(
        functools.partial(kernel, count, bond, width),
        out_shape=jax.ShapeDtypeStruct((nblock, width, width), jnp.bfloat16),
        in_specs=[
            in_smem, in_smem, in_place, in_place, in_place, in_place,
        ],
        out_specs=in_vmem,
        scratch_shapes=[
            pltpu.VMEM(psi.shape, jnp.bfloat16),
            pltpu.VMEM((bond, width, width), jnp.bfloat16),
            pltpu.VMEM(mpo.shape, jnp.bfloat16),
            pltpu.VMEM((SPREAD, depth, width), jnp.bfloat16),
            pltpu.VMEM((SPREAD, CAP * width, depth), jnp.bfloat16),
            pltpu.VMEM((width // SUB, padded, width), jnp.bfloat16),
            pltpu.VMEM((nblock, bond * SUB, padded), jnp.bfloat16),
            pltpu.VMEM((2, 2 * padded, CAP * width), jnp.bfloat16),
            pltpu.VMEM((nblock, width, width), jnp.bfloat16),
            pltpu.SMEM((CAP * SPREAD,), jnp.int32),
            pltpu.SemaphoreType.DMA((sends, CHUNKS)),
            pltpu.SemaphoreType.DMA((SPREAD, CHUNKS)),
            pltpu.SemaphoreType.DMA,
            pltpu.SemaphoreType.DMA((3,)),
        ],
        compiler_params=pltpu.CompilerParams(
            collective_id=0, has_side_effects=True, vmem_limit_bytes=60 * 1024 * 1024
        ),
        name="hamiltonian_product",
    )(
        block_target.reshape(nblock), block_phys, psi, left_env.reshape(bond, width, width),
        right_env.reshape(depth, width), mpo,
    )


def solution(mesh):
    in_specs = (
        P(("groups", "sector"), None, None),
        P(("groups", "sector"), None, None, None),
        P(("groups", "sector"), None, None, None),
        P("groups", None, None),
        P(("groups", "sector"), None),
        P(("groups", "sector")),
    )
    out_specs = P(("groups", "sector"), None, None)
    return jax.shard_map(
        functools.partial(per_device, mesh.shape["sector"]),
        mesh=mesh, in_specs=in_specs, out_specs=out_specs, check_vma=False,
    )
```
